512 devices in a mesh: ctx: 32 (over x, z_hi, core), dp: 16 (over z_lo, y).
Axes of the slice: x: 4, y: 4, z: 16 (z_hi: 4, z_lo: 4; z = z_hi * 4 + z_lo), core: 2. Of those that a mesh axis runs over, the one named last changes fastest.
Arguments:
- queries: bfloat16 [16, 8192, 2048], P('dp', 'ctx'), may hold values from -16 to 16
- keys: bfloat16 [16, 8192, 512], P('dp', 'ctx'), may hold values from -16 to 16
- values: bfloat16 [16, 8192, 512], P('dp', 'ctx'), may hold values from -6 to 6
- resid: bfloat16 [16, 8192, 2048], P('dp', 'ctx'), may hold values from -4 to 4
- out_weight: bfloat16 [2048, 2048], P('dp'), may hold values from -0.125 to 0.125
- head_weight: bfloat16 [2048, 200], P('dp'), may hold values from -0.125 to 0.125
- gain: bfloat16 [2048], P('dp'), may hold values from 0.5 to 1.5
- doc_ids: int32 [16, 8192], P('dp'), may hold values from 0 to 31, never falling along the last dimension, each value on 1 to 512 neighbouring positions
- prompt_lengths: int32 [16, 32], P('dp'), may hold values from 1 to 255
- targets: float32 [16, 8192], P('dp', 'ctx'), may hold values from -6 to 6
Outputs:
- quantiles: float32 [16, 8192, 200], P('dp', 'ctx')
- token_grad: bfloat16 [16, 8192, 2048], P('dp', 'ctx')
- grad_head: float32 [2048, 200], P('dp')
- grad_gain: float32 [2048], P('dp')
The draws below stay inside these ranges and needn't reach their ends.
Inputs may be any that keep to these rules, and one draw needn't show every extreme that they name: `doc_ids`: document numbers never fall along a sequence, and each document covers 1 to 512 positions.
All inputs are finite; a program needn't handle non-finite values.
Results may differ from the reference program's by a relative error of at most 0.018.
Values may be sent and summed in bfloat16 or wider, within the bound.
No kernel may reach another device: no remote copies, remote signals or barrier semaphores. Data moves between devices by JAX's collectives and lax.ppermute only.
A program may use at most 64 MiB of HBM per device.

```python
import math
import jax
import jax.numpy as jnp
import numpy as np
from jax import lax

D = 2048
QUERY_HEADS = 16
KEY_VALUE_HEADS = 4
HEAD_SIZE = 128
Q = 200
SPAN = 2
T_DEV = 256
PACKED_SEQUENCES = 16
PACKED_LENGTH = 8192
MOST = 512
COUNT = 32
N_CTX = 32


def draw_queries(key, part):
    key = jax.random.fold_in(key, 1)
    return jnp.clip(jax.random.normal(key, (PACKED_SEQUENCES, PACKED_LENGTH, QUERY_HEADS * HEAD_SIZE), jnp.float32), -4.0, 4.0).astype(jnp.bfloat16)


def draw_keys(key, part):
    key = jax.random.fold_in(key, 2)
    return jnp.clip(jax.random.normal(key, (PACKED_SEQUENCES, PACKED_LENGTH, KEY_VALUE_HEADS * HEAD_SIZE), jnp.float32), -4.0, 4.0).astype(jnp.bfloat16)


def with_ends(drawn, key, low, top_value):
    shape = drawn.shape
    index_at = [jax.random.randint(jax.random.fold_in(key, axis), (), 0, shape[axis]) for axis in range(len(shape))]
    drawn = drawn.at[tuple(index_at)].set(low)
    longest = shape.index(max(shape))
    index_at[longest] = (index_at[longest] + 1) % shape[longest]
    return drawn.at[tuple(index_at)].set(top_value)


def block_scale(own_key, extent, pieces, low, high):
    level = 1.0
    for position, shards_of in pieces:
        steps = jax.random.uniform(jax.random.fold_in(jax.random.fold_in(own_key, 6), position), (shards_of,), jnp.float32, low / len(pieces), high / len(pieces))
        level = level * jnp.repeat(jnp.exp(steps), extent[position] // shards_of).reshape((-1,) + (1,) * (len(extent) - 1 - position))
    return level


def length_profile(count, total, bound, skew):
    loads = [(1 << 20) // math.isqrt(standing ** skew) + 1 for standing in range(2, count + 1)]
    surplus, given = total - bound - (count - 1), [1] * (count - 1)
    while surplus > 0:
        movable = [i for i in range(count - 1) if given[i] < bound]
        mass, left = sum([loads[i] for i in movable]), surplus
        for i in movable:
            addition = min(bound - given[i], max(1, left * loads[i] // mass), surplus)
            given[i] = given[i] + addition
            surplus = surplus - addition
    return np.array([bound] + given)


def uneven(stream_key, count, total, most, skew):
    if count == 2:
        one = jax.random.randint(stream_key, (), max(1, total - most), min(most, total - 1) + 1)
        return jnp.stack([one, total - one])
    sizes = jnp.asarray(length_profile(count, total, most, skew), jnp.int32)
    couples = (count - 1) // 2
    giver, receiver = sizes[1:1 + 2 * couples:2], sizes[2:2 + 2 * couples:2]
    room = jnp.minimum(giver - 1, most - receiver)
    shifted = jax.random.randint(jax.random.fold_in(stream_key, 1), (couples,), 0, 1 << 20) % (room + 1)
    sizes = sizes.at[1:1 + 2 * couples:2].set(giver - shifted).at[2:2 + 2 * couples:2].set(receiver + shifted)
    return sizes[jax.random.permutation(jax.random.fold_in(stream_key, 2), count)]


def normal_values(rng, dims, deviation, most, shards=(), kind=jnp.bfloat16):
    level = block_scale(rng, dims, shards, -0.22, 0.18) if shards else 1.0
    entries = jax.random.normal(rng, dims, jnp.float32) * deviation * level
    return jnp.minimum(jnp.maximum(entries, -most), most).astype(kind)


def setup_inputs(seed: int = 0) -> dict:
    seeds = jax.random.split(jax.random.key(seed), 11)
    queries = draw_queries(jax.random.fold_in(seeds[10], 71), 0)
    keys = draw_keys(jax.random.fold_in(seeds[10], 71), 0)
    values = normal_values(seeds[2], (PACKED_SEQUENCES, PACKED_LENGTH, KEY_VALUE_HEADS * HEAD_SIZE), 1.0, 6.0, ((0, 16), (1, 32)))
    resid = normal_values(seeds[3], (PACKED_SEQUENCES, PACKED_LENGTH, D), 0.5, 4.0, ((0, 16), (1, 32)))
    out_weight = normal_values(seeds[4], (QUERY_HEADS * HEAD_SIZE, D), (QUERY_HEADS * HEAD_SIZE) ** -0.5, 0.125, ((0, 16),))
    head_weight = normal_values(seeds[5], (D, Q), D ** -0.5, 0.125, ((0, 16),))
    gain = jnp.clip(1.0 + 0.1 * jax.random.normal(seeds[6], (D,), jnp.float32), 0.5, 1.5).astype(jnp.bfloat16)
    doc_ids = jax.vmap(lambda own: jnp.searchsorted(jnp.cumsum(uneven(own, COUNT, PACKED_LENGTH, MOST, 1)), jnp.arange(PACKED_LENGTH), side="right"))(jax.random.split(seeds[7], PACKED_SEQUENCES)).reshape((PACKED_SEQUENCES, PACKED_LENGTH)).astype(jnp.int32)
    prompt_lengths = with_ends(jax.random.randint(seeds[8], (PACKED_SEQUENCES, COUNT), 1, MOST // 2), jax.random.fold_in(seeds[8], 1), 1, (MOST // 2) - 1).astype(jnp.int32)
    targets = normal_values(seeds[9], (PACKED_SEQUENCES, PACKED_LENGTH), 1.0, 6.0, ((0, 16), (1, 32)), jnp.float32)
    return dict(queries=queries, keys=keys, values=values, resid=resid, out_weight=out_weight, head_weight=head_weight, gain=gain, doc_ids=doc_ids, prompt_lengths=prompt_lengths, targets=targets)


NEGATIVE = -1e+30
EPSILON = 1e-05

def attend_block(query_matrix, key_span_rows, value_span_rows, query_ids, key_ids, query_pos, key_pos):
    row_total = query_matrix.shape[0]
    span_length = key_span_rows.shape[0]
    query_head_rows = query_matrix.reshape(row_total, KEY_VALUE_HEADS, QUERY_HEADS // KEY_VALUE_HEADS, HEAD_SIZE).transpose(1, 2, 0, 3)
    key_head_rows = key_span_rows.reshape(span_length, KEY_VALUE_HEADS, HEAD_SIZE).transpose(1, 0, 2)
    value_head_rows = value_span_rows.reshape(span_length, KEY_VALUE_HEADS, HEAD_SIZE).transpose(1, 0, 2)
    allowed = (query_ids[:, None] == key_ids[None, :]) & (key_pos[None, :] <= query_pos[:, None])

    def one_head(operands):
        query_group, key_head, value_head = operands
        scores = jnp.einsum('gtd,sd->gts', query_group.astype(jnp.float32), key_head.astype(jnp.float32)) * HEAD_SIZE ** (-0.5)
        scores = jnp.where(allowed[None], scores, NEGATIVE)
        top = lax.optimization_barrier(jnp.max(scores, axis=2, keepdims=True))
        weights = jnp.where(allowed[None], jnp.exp(scores - top), 0.0)
        probs = (weights / lax.optimization_barrier(jnp.sum(weights, axis=2, keepdims=True))).astype(jnp.bfloat16)
        mixed = jnp.einsum('gts,sd->gtd', probs.astype(jnp.float32), value_head.astype(jnp.float32))
        return mixed.astype(jnp.bfloat16)
    outputs = lax.map(one_head, (query_head_rows, key_head_rows, value_head_rows))
    return outputs.transpose(2, 0, 1, 3).reshape(row_total, QUERY_HEADS * HEAD_SIZE)

def head_pass(attended, resid_rows, out_weight, head_weight, gain, goals, live):
    projected = jnp.dot(attended, out_weight, preferred_element_type=jnp.float32)
    hidden = resid_rows.astype(jnp.float32) + projected
    rinv = lax.rsqrt(lax.optimization_barrier(jnp.mean(hidden * hidden, axis=1, keepdims=True)) + EPSILON)
    gain_f = gain.astype(jnp.float32)
    normed = (hidden * rinv * gain_f[None, :]).astype(jnp.bfloat16)
    theta = jnp.dot(normed, head_weight, preferred_element_type=jnp.float32)
    taus = (jnp.arange(theta.shape[1], dtype=jnp.float32) + 0.5) / theta.shape[1]
    gap = goals[:, None] - theta
    slope = jnp.abs(taus[None, :] - (gap < 0.0).astype(jnp.float32))
    dquant = (-live[:, None] * slope * jnp.clip(gap, -1.0, 1.0)).astype(jnp.bfloat16)
    dnormed = jnp.dot(dquant, head_weight.T, preferred_element_type=jnp.float32)
    scaled = dnormed * gain_f[None, :]
    inner = lax.optimization_barrier(jnp.mean(scaled * hidden, axis=1, keepdims=True))
    token_grad = (rinv * scaled - hidden * rinv * rinv * rinv * inner).astype(jnp.bfloat16)
    head_term = jnp.dot(normed.T, dquant, preferred_element_type=jnp.float32)
    gain_term = lax.optimization_barrier(jnp.sum(dnormed * hidden * rinv, axis=0))
    return (theta, token_grad, head_term, gain_term)

def live_mask(ids_row, local_ids, prompts, positions):
    docs = jnp.arange(prompts.shape[0], dtype=jnp.int32)
    starts = lax.optimization_barrier(jnp.sum((ids_row[None, :] < docs[:, None]).astype(jnp.int32), axis=1))
    onehot = (local_ids[:, None] == docs[None, :]).astype(jnp.int32)
    own_start = lax.optimization_barrier(jnp.sum(onehot * starts[None, :], axis=1))
    own_prompt = lax.optimization_barrier(jnp.sum(onehot * prompts[None, :], axis=1))
    return (positions - own_start >= own_prompt).astype(jnp.float32)

def reference(queries, keys, values, resid, out_weight, head_weight, gain, doc_ids, prompt_lengths, targets):
    reach_rows = SPAN * T_DEV

    def one_sequence(operands):
        query_seq, key_seq, value_seq, resid_seq, ids_row, prompts, goals = operands
        padded_keys = jnp.concatenate([jnp.zeros((reach_rows, key_seq.shape[1]), key_seq.dtype), key_seq], axis=0)
        padded_values = jnp.concatenate([jnp.zeros((reach_rows, value_seq.shape[1]), value_seq.dtype), value_seq], axis=0)
        padded_ids = jnp.concatenate([jnp.full((reach_rows,), -1, jnp.int32), ids_row])

        def one_block(block):
            first_row = (block * T_DEV).astype(jnp.int32)
            query_matrix = lax.dynamic_slice_in_dim(query_seq, first_row, T_DEV, 0)
            key_span_rows = lax.dynamic_slice_in_dim(padded_keys, first_row, reach_rows + T_DEV, 0)
            value_span_rows = lax.dynamic_slice_in_dim(padded_values, first_row, reach_rows + T_DEV, 0)
            key_ids = lax.dynamic_slice_in_dim(padded_ids, first_row, reach_rows + T_DEV, 0)
            query_ids = lax.dynamic_slice_in_dim(ids_row, first_row, T_DEV, 0)
            query_pos = first_row + jnp.arange(T_DEV, dtype=jnp.int32)
            key_pos = first_row - reach_rows + jnp.arange(reach_rows + T_DEV, dtype=jnp.int32)
            return attend_block(query_matrix, key_span_rows, value_span_rows, query_ids, key_ids, query_pos, key_pos)
        attended = lax.map(one_block, jnp.arange(N_CTX, dtype=jnp.int32)).reshape(PACKED_LENGTH, QUERY_HEADS * HEAD_SIZE)
        positions = jnp.arange(PACKED_LENGTH, dtype=jnp.int32)
        live = live_mask(ids_row, ids_row, prompts, positions)
        return head_pass(attended, resid_seq, out_weight, head_weight, gain, goals, live)
    theta, token_grad, head_terms, gain_terms = lax.map(one_sequence, (queries, keys, values, resid, doc_ids, prompt_lengths, targets))
    grad_head = lax.optimization_barrier(jnp.sum(head_terms, axis=0)) / PACKED_LENGTH
    grad_gain = lax.optimization_barrier(jnp.sum(gain_terms, axis=0)) / PACKED_LENGTH
    return (theta, token_grad, grad_head, grad_gain)
```

```python
import math

import jax
import jax.numpy as jnp
from jax import lax
from jax.experimental import pallas as pl
from jax.experimental.pallas import tpu as pltpu
from jax.sharding import Mesh, PartitionSpec as P

AXES = ("x", "zh", "core", "zl", "y")
EXTENT = (4, 4, 2, 4, 4)
QUERY_HEADS = 16
KV_HEADS = 4
HEAD_SIZE = 128
SPAN = 2
WIDTH = 2048
QUANTILES = 200
EPSILON = 1e-05
NEGATIVE = -1e30
PARTS = 8
REAL = QUANTILES // PARTS
ROWS = 32
CHUNK = WIDTH // PARTS
BLOCK = 128 + 16


def attend_kernel(q_ref, k0_ref, k1_ref, k2_ref, v0_ref, v1_ref, v2_ref, bias_ref, out_ref):
    keys = jnp.concatenate([k0_ref[...], k1_ref[...], k2_ref[...]], axis=0)
    values = jnp.concatenate([v0_ref[...], v1_ref[...], v2_ref[...]], axis=0)
    bias = bias_ref[...]
    factor = HEAD_SIZE**-0.5 * math.log2(math.e)
    for member in range(QUERY_HEADS // KV_HEADS):
        q = q_ref[:, member * HEAD_SIZE : (member + 1) * HEAD_SIZE]
        scores = lax.dot_general(q, keys, (((1,), (1,)), ((), ())), preferred_element_type=jnp.float32)
        scores = scores + bias
        top = jnp.max(scores, axis=1, keepdims=True)
        weights = jnp.exp2((scores - top) * factor)
        total = jnp.sum(weights, axis=1, keepdims=True)
        mixed = jnp.dot(weights.astype(jnp.bfloat16), values, preferred_element_type=jnp.float32)
        out_ref[member] = (mixed / total).astype(jnp.bfloat16)


def attend(queries, own, near, far, bias):
    rows = queries.shape[0]
    one = (rows, HEAD_SIZE)
    key_spec = pl.BlockSpec(one, lambda g: (0, g))
    value_spec = pl.BlockSpec(one, lambda g: (0, g + KV_HEADS))
    return pl.pallas_call(
        attend_kernel,
        grid=(KV_HEADS,),
        in_specs=[pl.BlockSpec((rows, 4 * HEAD_SIZE), lambda g: (0, g))]
        + [key_spec] * 3
        + [value_spec] * 3
        + [pl.BlockSpec(bias.shape, lambda g: (0, 0))],
        out_specs=pl.BlockSpec((4, rows, HEAD_SIZE), lambda g: (0, 0, g)),
        out_shape=jax.ShapeDtypeStruct((4, rows, KV_HEADS * HEAD_SIZE), jnp.bfloat16),
        compiler_params=pltpu.CompilerParams(vmem_limit_bytes=40 * 2**20),
        cost_estimate=pl.CostEstimate(flops=16 * 256 * 768 * 128 * 4, bytes_accessed=4 * 2**20, transcendentals=16 * 256 * 768),
    )(queries, far, near, own, far, near, own, bias)


def head_kernel(
    att_ref, weight_ref, resid_ref, goals_ref, live_ref, tau_ref, real_ref,
    theta_ref, token_ref, share_ref, hidden_ref, head_ref, normed_ref,
):
    step = pl.program_id(0)
    blocks = [(y, z) for y in range(4) for z in range(4)]
    weight = jnp.concatenate([weight_ref[0, 0, y, z, :128, :] for y, z in blocks], axis=0)
    att = jnp.concatenate([att_ref[y] for y in range(4)], axis=1)
    part = jnp.dot(att, weight, preferred_element_type=jnp.float32)
    hidden_ref[step] = part + resid_ref[...].astype(jnp.float32)
    place = (step % 2) * 4 + step // 2
    for y, z in blocks:
        extra = weight_ref[0, 0, y, z, 128:, :]
        rows = jnp.concatenate([extra[:, :128], extra[:, 128:]], axis=0)
        head_ref[place, :, (z * 4 + y) * 128 : (z * 4 + y + 1) * 128] = rows

    @pl.when(step == PARTS - 1)
    def _():
        count = hidden_ref.shape[1]
        squares = jnp.zeros((count, CHUNK), jnp.float32)
        for i in range(PARTS):
            squares = squares + hidden_ref[i] * hidden_ref[i]
        rinv = lax.rsqrt(jnp.sum(squares, axis=1, keepdims=True) / WIDTH + EPSILON)
        gains = []
        theta = jnp.zeros((PARTS * ROWS, count), jnp.float32)
        for i in range(PARTS):
            cols = slice(i * CHUNK, (i + 1) * CHUNK)
            gain = head_ref[0, :, cols].astype(jnp.float32)[REAL : REAL + 1, :]
            gains.append(gain)
            normed = (hidden_ref[i] * rinv * gain).astype(jnp.bfloat16)
            normed_ref[i] = normed
            head = head_ref[:, :, cols].reshape(PARTS * ROWS, CHUNK)
            theta = theta + lax.dot_general(head, normed, (((1,), (1,)), ((), ())), preferred_element_type=jnp.float32)
        for b in range(PARTS):
            theta_ref[b * REAL : (b + 1) * REAL, :] = theta[b * ROWS : b * ROWS + REAL, :]
        gap = goals_ref[...] - theta
        slope = jnp.abs(tau_ref[...] - jnp.where(gap < 0.0, 1.0, 0.0))
        dquant = -live_ref[...] * slope * jnp.clip(gap, -1.0, 1.0)
        dquant = jnp.where(real_ref[...] > 0.0, dquant, 0.0).astype(jnp.bfloat16)
        inner = jnp.zeros((count, CHUNK), jnp.float32)
        scaled = []
        row = lax.broadcasted_iota(jnp.int32, (PARTS * ROWS, CHUNK), 0)
        for i in range(PARTS):
            cols = slice(i * CHUNK, (i + 1) * CHUNK)
            head = head_ref[:, :, cols].reshape(PARTS * ROWS, CHUNK)
            dnormed = lax.dot_general(dquant, head, (((0,), (0,)), ((), ())), preferred_element_type=jnp.float32)
            product = dnormed * hidden_ref[i]
            inner = inner + product * gains[i]
            gain_term = jnp.sum(product * rinv, axis=0, keepdims=True)
            term = jnp.dot(dquant, normed_ref[i], preferred_element_type=jnp.float32)
            term = jnp.where(row == REAL, gain_term, term) * (1.0 / 8192)
            term = term.astype(jnp.bfloat16).reshape(2, 4, ROWS, CHUNK)
            for half in range(2):
                j = 2 * i + half
                share_ref[:, :, j % 4, j // 4] = term[:, :, :, half * 128 : (half + 1) * 128]
            scaled.append(dnormed * gains[i])
        mean = jnp.sum(inner, axis=1, keepdims=True) / WIDTH
        back = rinv * rinv * rinv * mean
        for i in range(PARTS):
            cols = slice(i * CHUNK, (i + 1) * CHUNK)
            token_ref[:, cols] = (rinv * scaled[i] - hidden_ref[i] * back).astype(jnp.bfloat16)


def head_pass(attended, weights, resid, goals, live):
    rows = resid.shape[0]
    index = jnp.arange(PARTS * ROWS, dtype=jnp.int32)
    inside = index % ROWS
    tau = ((index // ROWS * REAL + inside).astype(jnp.float32) + 0.5) / QUANTILES
    real = (inside < REAL).astype(jnp.float32)
    whole = lambda shape: pl.BlockSpec(shape, lambda s: (0,) * len(shape))
    column = (PARTS * ROWS, 1)
    return pl.pallas_call(
        head_kernel,
        grid=(PARTS,),
        in_specs=[
            whole(attended.shape),
            pl.BlockSpec((1, 1, 4, 4, BLOCK, CHUNK), lambda s: (s // 2, s % 2, 0, 0, 0, 0)),
            pl.BlockSpec((rows, CHUNK), lambda s: (0, s)),
            whole((1, rows)),
            whole((1, rows)),
            whole(column),
            whole(column),
        ],
        out_specs=[
            whole((QUANTILES, rows)),
            whole((rows, WIDTH)),
            whole((2, 4, 4, 4, ROWS, 128)),
        ],
        out_shape=[
            jax.ShapeDtypeStruct((QUANTILES, rows), jnp.float32),
            jax.ShapeDtypeStruct((rows, WIDTH), jnp.bfloat16),
            jax.ShapeDtypeStruct((2, 4, 4, 4, ROWS, 128), jnp.bfloat16),
        ],
        scratch_shapes=[
            pltpu.VMEM((PARTS, rows, CHUNK), jnp.float32),
            pltpu.VMEM((PARTS, ROWS, WIDTH), jnp.bfloat16),
            pltpu.VMEM((PARTS, rows, CHUNK), jnp.bfloat16),
        ],
        compiler_params=pltpu.CompilerParams(vmem_limit_bytes=48 * 2**20),
        cost_estimate=pl.CostEstimate(flops=3 * 10**9, bytes_accessed=13 * 2**20, transcendentals=0),
    )(attended, weights, resid, goals, live, tau[:, None], real[:, None])


def exchange(value, axes):
    return lax.all_to_all(value, axes, 0, 0, tiled=False)


def ring(value, axes, count, steps):
    return lax.ppermute(value, axes, [(i, (i + steps) % count) for i in range(count)])


def total(pieces):
    return jnp.sum(pieces.astype(jnp.float32), axis=0)


def gather_weights(out_weight, head_weight, gain):
    x, core = lax.axis_index("x"), lax.axis_index("core")
    columns = lax.dynamic_slice_in_dim(out_weight, (x * 2 + core) * CHUNK, CHUNK, axis=1)
    block = core * 4 + x
    head_rows = lax.dynamic_slice_in_dim(head_weight.T, block * REAL, REAL, axis=0)
    gain_row = jnp.where(block == 0, gain, jnp.zeros_like(gain))[None, :]
    rest = jnp.zeros((ROWS - REAL - 1, 128), jnp.bfloat16)
    packed = jnp.concatenate([head_rows, gain_row, rest], axis=0)
    packed = jnp.concatenate([packed[:16], packed[16:]], axis=1)
    mine = jnp.concatenate([columns, packed], axis=0)
    along_z = exchange(jnp.broadcast_to(mine[None], (4,) + mine.shape), "zl")
    gathered = lax.all_gather(along_z, ("x", "core", "y"), axis=0, tiled=False)
    return gathered.reshape(4, 2, 4, 4, BLOCK, CHUNK)


def reduce_shares(share):
    both = total(exchange(share, "core")).astype(jnp.bfloat16)
    plane = total(exchange(both.reshape(16, 4, ROWS, 128), ("x", "y"))).astype(jnp.bfloat16)
    spread = jnp.broadcast_to(plane[None], (4, 4, ROWS, 128)).reshape(16, ROWS, 128)
    line = total(exchange(spread, ("zh", "zl"))).astype(jnp.bfloat16)
    parts = exchange(jnp.broadcast_to(line[None], (PARTS, ROWS, 128)), ("x", "core"))
    parts = parts.reshape(4, 2, ROWS, 128).transpose(1, 0, 2, 3).astype(jnp.float32)
    grad_head = parts[:, :, :REAL].reshape(QUANTILES, 128).T
    return grad_head, parts[0, 0, REAL]


def local(queries, keys, values, resid, out_weight, head_weight, gain, doc_ids, prompt_lengths, targets):
    rows = queries.shape[1]
    core = lax.axis_index("core")
    place = (lax.axis_index("x") * 4 + lax.axis_index("zh")) * 2 + core
    own = jnp.concatenate([keys[0], values[0]], axis=1)
    far = ring(own, ("x", "zh"), 16, 1)
    weights = gather_weights(out_weight, head_weight, gain)
    near = ring(jnp.where(core == 0, own, far), "core", 2, 1)

    ids = doc_ids[0]
    first = place * rows
    query_ids = lax.dynamic_slice_in_dim(ids, first, rows)
    docs = jnp.arange(prompt_lengths.shape[1], dtype=jnp.int32)
    starts = jnp.sum((ids[None, :] < docs[:, None]).astype(jnp.int32), axis=1)
    onehot = (query_ids[:, None] == docs[None, :]).astype(jnp.int32)
    own_start = jnp.sum(onehot * starts[None, :], axis=1)
    own_prompt = jnp.sum(onehot * prompt_lengths[0][None, :], axis=1)
    query_pos = first + jnp.arange(rows, dtype=jnp.int32)
    live = (query_pos - own_start >= own_prompt).astype(jnp.float32)
    key_pos = first - SPAN * rows + jnp.arange((SPAN + 1) * rows, dtype=jnp.int32)
    allowed = (key_pos[None, :] >= own_start[:, None]) & (key_pos[None, :] <= query_pos[:, None])
    bias = jnp.where(allowed, 0.0, NEGATIVE).astype(jnp.float32)

    attended = attend(queries[0], own, near, far, bias)
    theta, token_grad, share = head_pass(attended, weights, resid[0], targets, live[None, :])
    grad_head, grad_gain = reduce_shares(share)
    return theta.T[None], token_grad[None], grad_head, grad_gain


def solution(mesh):
    fine = Mesh(mesh.devices.reshape(EXTENT), AXES)
    ctx, dp = ("x", "zh", "core"), ("zl", "y")
    in_specs = (
        P(dp, ctx, None),
        P(dp, ctx, None),
        P(dp, ctx, None),
        P(dp, ctx, None),
        P(dp, None),
        P(dp, None),
        P(dp),
        P(dp, None),
        P(dp, None),
        P(dp, ctx),
    )
    out_specs = (P(dp, ctx, None), P(dp, ctx, None), P(dp, None), P(dp))
    return jax.shard_map(local, mesh=fine, in_specs=in_specs, out_specs=out_specs, check_vma=False)
```

```python
import math

import jax
import jax.numpy as jnp
from jax import lax
from jax.experimental import pallas as pl
from jax.experimental.pallas import tpu as pltpu
from jax.sharding import Mesh, PartitionSpec as P

AXES = ("x", "zh", "core", "zl", "y")
EXTENT = (4, 4, 2, 4, 4)
QUERY_HEADS = 16
KV_HEADS = 4
HEAD_SIZE = 128
SPAN = 2
WIDTH = 2048
QUANTILES = 200
EPSILON = 1e-05
NEGATIVE = -1e30
PARTS = 8
REAL = QUANTILES // PARTS
ROWS = 32
CHUNK = WIDTH // PARTS
BLOCK = 128 + 16


def attend_kernel(q_ref, k0_ref, k1_ref, k2_ref, v0_ref, v1_ref, v2_ref, bias_ref, out_ref):
    keys = jnp.concatenate([k0_ref[...], k1_ref[...], k2_ref[...]], axis=0)
    values = jnp.concatenate([v0_ref[...], v1_ref[...], v2_ref[...]], axis=0)
    bias = bias_ref[...]
    factor = HEAD_SIZE**-0.5 * math.log2(math.e)
    for member in range(QUERY_HEADS // KV_HEADS):
        q = q_ref[:, member * HEAD_SIZE : (member + 1) * HEAD_SIZE]
        scores = lax.dot_general(q, keys, (((1,), (1,)), ((), ())), preferred_element_type=jnp.float32)
        scores = scores + bias
        top = jnp.max(scores, axis=1, keepdims=True)
        weights = jnp.exp2((scores - top) * factor)
        total = jnp.sum(weights, axis=1, keepdims=True)
        mixed = jnp.dot(weights.astype(jnp.bfloat16), values, preferred_element_type=jnp.float32)
        out_ref[member] = (mixed / total).astype(jnp.bfloat16)


def attend(queries, first, own, near, far, bias):
    rows = queries.shape[0]
    heads = own.shape[1] // (2 * HEAD_SIZE)
    one = (rows, HEAD_SIZE)
    key_spec = pl.BlockSpec(one, lambda g: (0, g))
    value_spec = pl.BlockSpec(one, lambda g: (0, g + heads))
    return pl.pallas_call(
        attend_kernel,
        grid=(heads,),
        in_specs=[pl.BlockSpec((rows, 4 * HEAD_SIZE), lambda g: (0, g + first))]
        + [key_spec] * 3
        + [value_spec] * 3
        + [pl.BlockSpec(bias.shape, lambda g: (0, 0))],
        out_specs=pl.BlockSpec((4, rows, HEAD_SIZE), lambda g: (0, 0, g)),
        out_shape=jax.ShapeDtypeStruct((4, rows, heads * HEAD_SIZE), jnp.bfloat16),
        compiler_params=pltpu.CompilerParams(vmem_limit_bytes=40 * 2**20),
        cost_estimate=pl.CostEstimate(
            flops=4 * heads * 256 * 768 * 128 * 4, bytes_accessed=heads * 2**20, transcendentals=4 * heads * 256 * 768
        ),
    )(queries, far, near, own, far, near, own, bias)


def head_kernel(
    core_ref, *refs
):
    att_refs, own_refs, other_refs = refs[:1], refs[1:5], refs[5:9]
    resid_ref, goals_ref, live_ref, tau_ref, real_ref, theta_ref, token_ref, share_ref, hidden_ref, head_ref, normed_ref = refs[9:]
    step = pl.program_id(0)
    core = core_ref[0]
    att = jnp.concatenate([ref[y] for y in range(4) for ref in att_refs], axis=1)
    blocks = [(y, z) for y in range(4) for z in range(4)]
    for index, weight_refs in ((core, own_refs), (1 - core, other_refs)):
        part = step * 2 + index
        place = index * 4 + step
        weight = jnp.concatenate([weight_refs[y][0, z, :128, :] for y, z in blocks], axis=0)
        projected = jnp.dot(att, weight, preferred_element_type=jnp.float32)
        resid = resid_ref[:, pl.ds(pl.multiple_of(part * CHUNK, CHUNK), CHUNK)]
        hidden_ref[part] = projected + resid.astype(jnp.float32)
        for y, z in blocks:
            extra = weight_refs[y][0, z, 128:, :]
            rows = jnp.concatenate([extra[:, :128], extra[:, 128:]], axis=0)
            head_ref[place, :, (z * 4 + y) * 128 : (z * 4 + y + 1) * 128] = rows

    @pl.when(step == 3)
    def _():
        count = hidden_ref.shape[1]
        squares = jnp.zeros((count, CHUNK), jnp.float32)
        for i in range(PARTS):
            squares = squares + hidden_ref[i] * hidden_ref[i]
        rinv = lax.rsqrt(jnp.sum(squares, axis=1, keepdims=True) / WIDTH + EPSILON)
        gains = []
        theta = jnp.zeros((PARTS * ROWS, count), jnp.float32)
        for i in range(PARTS):
            cols = slice(i * CHUNK, (i + 1) * CHUNK)
            gain = head_ref[0, :, cols].astype(jnp.float32)[REAL : REAL + 1, :]
            gains.append(gain)
            normed = (hidden_ref[i] * rinv * gain).astype(jnp.bfloat16)
            normed_ref[i] = normed
            head = head_ref[:, :, cols].reshape(PARTS * ROWS, CHUNK)
            theta = theta + lax.dot_general(head, normed, (((1,), (1,)), ((), ())), preferred_element_type=jnp.float32)
        for b in range(PARTS):
            theta_ref[b * REAL : (b + 1) * REAL, :] = theta[b * ROWS : b * ROWS + REAL, :]
        gap = goals_ref[...] - theta
        slope = jnp.abs(tau_ref[...] - jnp.where(gap < 0.0, 1.0, 0.0))
        dquant = -live_ref[...] * slope * jnp.clip(gap, -1.0, 1.0)
        dquant = jnp.where(real_ref[...] > 0.0, dquant, 0.0).astype(jnp.bfloat16)
        inner = jnp.zeros((count, CHUNK), jnp.float32)
        scaled = []
        row = lax.broadcasted_iota(jnp.int32, (PARTS * ROWS, CHUNK), 0)
        for i in range(PARTS):
            cols = slice(i * CHUNK, (i + 1) * CHUNK)
            head = head_ref[:, :, cols].reshape(PARTS * ROWS, CHUNK)
            dnormed = lax.dot_general(dquant, head, (((0,), (0,)), ((), ())), preferred_element_type=jnp.float32)
            product = dnormed * hidden_ref[i]
            inner = inner + product * gains[i]
            gain_term = jnp.sum(product * rinv, axis=0, keepdims=True)
            term = jnp.dot(dquant, normed_ref[i], preferred_element_type=jnp.float32)
            term = jnp.where(row == REAL, gain_term, term) * (1.0 / 8192)
            term = term.astype(jnp.bfloat16).reshape(2, 4, ROWS, CHUNK)
            for half in range(2):
                j = 2 * i + half
                share_ref[:, :, j % 4, j // 4] = term[:, :, :, half * 128 : (half + 1) * 128]
            scaled.append(dnormed * gains[i])
        mean = jnp.sum(inner, axis=1, keepdims=True) / WIDTH
        back = rinv * rinv * rinv * mean
        for i in range(PARTS):
            cols = slice(i * CHUNK, (i + 1) * CHUNK)
            token_ref[:, cols] = (rinv * scaled[i] - hidden_ref[i] * back).astype(jnp.bfloat16)


def head_pass(core, attended, own, other, resid, goals, live):
    rows = resid.shape[0]
    index = jnp.arange(PARTS * ROWS, dtype=jnp.int32)
    inside = index % ROWS
    tau = ((index // ROWS * REAL + inside).astype(jnp.float32) + 0.5) / QUANTILES
    real = (inside < REAL).astype(jnp.float32)
    whole = lambda shape: pl.BlockSpec(shape, lambda s, c: (0,) * len(shape))
    column = (PARTS * ROWS, 1)
    slot = lambda s, y, c: c * (s * 4 + y) + (1 - c) * (y * 4 + s)
    block = (1, 4, BLOCK, CHUNK)
    own_specs = [pl.BlockSpec(block, lambda s, c, y=y: (slot(s, y, c[0]), 0, 0, 0)) for y in range(4)]
    other_specs = [pl.BlockSpec(block, lambda s, c, y=y: (slot(s, y, 1 - c[0]), 0, 0, 0)) for y in range(4)]
    return pl.pallas_call(
        head_kernel,
        grid_spec=pltpu.PrefetchScalarGridSpec(
            num_scalar_prefetch=1,
            grid=(4,),
            in_specs=[whole(a.shape) for a in attended]
            + own_specs
            + other_specs
            + [whole((rows, WIDTH)), whole((1, rows)), whole((1, rows)), whole(column), whole(column)],
            out_specs=[whole((QUANTILES, rows)), whole((rows, WIDTH)), whole((2, 4, 4, 4, ROWS, 128))],
            scratch_shapes=[
                pltpu.VMEM((PARTS, rows, CHUNK), jnp.float32),
                pltpu.VMEM((PARTS, ROWS, WIDTH), jnp.bfloat16),
                pltpu.VMEM((PARTS, rows, CHUNK), jnp.bfloat16),
            ],
        ),
        out_shape=[
            jax.ShapeDtypeStruct((QUANTILES, rows), jnp.float32),
            jax.ShapeDtypeStruct((rows, WIDTH), jnp.bfloat16),
            jax.ShapeDtypeStruct((2, 4, 4, 4, ROWS, 128), jnp.bfloat16),
        ],
        compiler_params=pltpu.CompilerParams(vmem_limit_bytes=48 * 2**20),
        cost_estimate=pl.CostEstimate(flops=3 * 10**9, bytes_accessed=13 * 2**20, transcendentals=0),
    )(core[None], *attended, *[own] * 4, *[other] * 4, resid, goals, live, tau[:, None], real[:, None])


def exchange(value, axes):
    return lax.all_to_all(value, axes, 0, 0, tiled=False)


def plane_groups(mixed):
    place = lambda x, h, c, z, y: (((x * 4 + h) * 2 + c) * 4 + z) * 4 + y
    groups = []
    for h in range(4):
        for c in range(2):
            for z in range(4):
                for i in range(4):
                    if (c == 0) == mixed:
                        groups.append([place(k, h, c, z, i) for k in range(4)])
                    else:
                        groups.append([place(i, h, c, z, k) for k in range(4)])
    return groups


def spread(value, first):
    copies = jnp.broadcast_to(value[None], (4,) + value.shape)
    return lax.all_to_all(copies, AXES, 0, 0, axis_index_groups=plane_groups(first), tiled=False)


def ring(value, axes, count, steps):
    return lax.ppermute(value, axes, [(i, (i + steps) % count) for i in range(count)])


def total(pieces):
    return jnp.sum(pieces.astype(jnp.float32), axis=0)


def gather_weights(out_weight, head_weight, gain, packed_kv, ready):
    x, core = lax.axis_index("x"), lax.axis_index("core")
    columns = lax.dynamic_slice_in_dim(out_weight, (x * 2 + core) * CHUNK, CHUNK, axis=1)
    block = core * 4 + x
    head_rows = lax.dynamic_slice_in_dim(head_weight.T, block * REAL, REAL, axis=0)
    gain_row = jnp.where(block == 0, gain, jnp.zeros_like(gain))[None, :]
    rest = jnp.zeros((ROWS - REAL - 1, 128), jnp.bfloat16)
    packed = jnp.concatenate([head_rows, gain_row, rest], axis=0)
    packed = jnp.concatenate([packed[:16], packed[16:]], axis=1)
    mine = jnp.concatenate([columns, packed], axis=0)
    def passed(piece):
        return spread(spread(piece, True), False).reshape(16, 4, BLOCK, CHUNK)

    along_z = exchange(jnp.broadcast_to(mine[None], (4,) + mine.shape), "zl")
    along_z, packed_kv = lax.optimization_barrier((along_z, packed_kv))
    far = ring(packed_kv, ("x", "zh"), 16, 1)
    own = lax.cond(ready, passed, lambda piece: jnp.zeros((16, 4, BLOCK, CHUNK), jnp.bfloat16), along_z)
    own, far = lax.optimization_barrier((own, far))
    return own, ring(own, "core", 2, 1), far


def reduce_shares(share):
    both = total(exchange(share, "core")).astype(jnp.bfloat16)
    plane = total(exchange(both.reshape(16, 4, ROWS, 128), ("x", "y"))).astype(jnp.bfloat16)
    spread = jnp.broadcast_to(plane[None], (4, 4, ROWS, 128)).reshape(16, ROWS, 128)
    line = total(exchange(spread, ("zh", "zl"))).astype(jnp.bfloat16)
    parts = exchange(jnp.broadcast_to(line[None], (PARTS, ROWS, 128)), ("x", "core"))
    parts = parts.reshape(4, 2, ROWS, 128).transpose(1, 0, 2, 3).astype(jnp.float32)
    grad_head = parts[:, :, :REAL].reshape(QUANTILES, 128).T
    return grad_head, parts[0, 0, REAL]


def local(queries, keys, values, resid, out_weight, head_weight, gain, doc_ids, prompt_lengths, targets):
    rows = queries.shape[1]
    core = lax.axis_index("core")
    place = (lax.axis_index("x") * 4 + lax.axis_index("zh")) * 2 + core
    own = jnp.concatenate([keys[0], values[0]], axis=1)
    mine, other, far = gather_weights(out_weight, head_weight, gain, own, doc_ids[0, 0] >= 0)
    near = ring(jnp.where(core == 0, own, far), "core", 2, 1)

    ids = doc_ids[0]
    first = place * rows
    query_ids = lax.dynamic_slice_in_dim(ids, first, rows)
    docs = jnp.arange(prompt_lengths.shape[1], dtype=jnp.int32)
    starts = jnp.sum((ids[None, :] < docs[:, None]).astype(jnp.int32), axis=1)
    onehot = (query_ids[:, None] == docs[None, :]).astype(jnp.int32)
    own_start = jnp.sum(onehot * starts[None, :], axis=1)
    own_prompt = jnp.sum(onehot * prompt_lengths[0][None, :], axis=1)
    query_pos = first + jnp.arange(rows, dtype=jnp.int32)
    live = (query_pos - own_start >= own_prompt).astype(jnp.float32)
    key_pos = first - SPAN * rows + jnp.arange((SPAN + 1) * rows, dtype=jnp.int32)
    allowed = (key_pos[None, :] >= own_start[:, None]) & (key_pos[None, :] <= query_pos[:, None])
    bias = jnp.where(allowed, 0.0, NEGATIVE).astype(jnp.float32)

    attended = [attend(queries[0], 0, own, near, far, bias)]
    theta, token_grad, share = head_pass(core, attended, mine, other, resid[0], targets, live[None, :])
    grad_head, grad_gain = reduce_shares(share)
    return theta.T[None], token_grad[None], grad_head, grad_gain


def solution(mesh):
    fine = Mesh(mesh.devices.reshape(EXTENT), AXES)
    ctx, dp = ("x", "zh", "core"), ("zl", "y")
    in_specs = (
        P(dp, ctx, None),
        P(dp, ctx, None),
        P(dp, ctx, None),
        P(dp, ctx, None),
        P(dp, None),
        P(dp, None),
        P(dp),
        P(dp, None),
        P(dp, None),
        P(dp, ctx),
    )
    out_specs = (P(dp, ctx, None), P(dp, ctx, None), P(dp, None), P(dp))
    return jax.shard_map(local, mesh=fine, in_specs=in_specs, out_specs=out_specs, check_vma=False)
```

```python
import math

import jax
import jax.numpy as jnp
from jax import lax
from jax.experimental import pallas as pl
from jax.experimental.pallas import tpu as pltpu
from jax.sharding import Mesh, PartitionSpec as P

AXES = ("x", "zh", "core", "zl", "y")
EXTENT = (4, 4, 2, 4, 4)
QUERY_HEADS = 16
KV_HEADS = 4
HEAD_SIZE = 128
SPAN = 2
WIDTH = 2048
QUANTILES = 200
EPSILON = 1e-05
NEGATIVE = -1e30
PARTS = 8
REAL = QUANTILES // PARTS
ROWS = 32
CHUNK = WIDTH // PARTS
BLOCK = 128 + 16


def attend_kernel(q_ref, k0_ref, k1_ref, k2_ref, v0_ref, v1_ref, v2_ref, bias_ref, out_ref):
    keys = jnp.concatenate([k0_ref[...], k1_ref[...], k2_ref[...]], axis=0)
    values = jnp.concatenate([v0_ref[...], v1_ref[...], v2_ref[...]], axis=0)
    values = jnp.concatenate([values, jnp.ones(values.shape, values.dtype)], axis=1)
    factor = HEAD_SIZE**-0.5 * math.log2(math.e)
    members = QUERY_HEADS // KV_HEADS
    rows = q_ref.shape[0] // 2
    reach = keys.shape[0] - rows
    jobs = [(m, h * rows) for m in range(members) for h in range(2)]
    scores = []
    for member, row in jobs:
        q = q_ref[row : row + rows, member * HEAD_SIZE : (member + 1) * HEAD_SIZE]
        product = lax.dot_general(q, keys[row : row + reach], (((1,), (1,)), ((), ())), preferred_element_type=jnp.float32)
        scores.append(product + bias_ref[row : row + rows, row : row + reach])
    weights = [jnp.exp2((s - jnp.max(s, axis=1, keepdims=True)) * factor).astype(jnp.bfloat16) for s in scores]
    for (member, row), weight in zip(jobs, weights):
        mixed = jnp.dot(weight, values[row : row + reach], preferred_element_type=jnp.float32)
        mixed = mixed[:, :HEAD_SIZE] / mixed[:, HEAD_SIZE:]
        out_ref[member, row : row + rows] = mixed.astype(jnp.bfloat16)


def attend(queries, first, own, near, far, bias):
    rows = queries.shape[0]
    heads = own.shape[1] // (2 * HEAD_SIZE)
    one = (rows, HEAD_SIZE)
    key_spec = pl.BlockSpec(one, lambda g: (0, g))
    value_spec = pl.BlockSpec(one, lambda g: (0, g + heads))
    return pl.pallas_call(
        attend_kernel,
        grid=(heads,),
        in_specs=[pl.BlockSpec((rows, 4 * HEAD_SIZE), lambda g: (0, g + first))]
        + [key_spec] * 3
        + [value_spec] * 3
        + [pl.BlockSpec(bias.shape, lambda g: (0, 0))],
        out_specs=pl.BlockSpec((4, rows, HEAD_SIZE), lambda g: (0, 0, g)),
        out_shape=jax.ShapeDtypeStruct((4, rows, heads * HEAD_SIZE), jnp.bfloat16),
        compiler_params=pltpu.CompilerParams(vmem_limit_bytes=16 * 2**20),
        cost_estimate=pl.CostEstimate(
            flops=4 * heads * 256 * 768 * 128 * 4, bytes_accessed=heads * 2**20, transcendentals=4 * heads * 256 * 768
        ),
    )(queries, far, near, own, far, near, own, bias)


def head_kernel(
    core_ref, *refs
):
    att_refs, own_refs, other_refs = refs[:1], refs[1:5], refs[5:9]
    resid_ref, goals_ref, live_ref, tau_ref, real_ref, theta_ref, token_ref, share_ref, hidden_ref, head_ref, normed_ref = refs[9:]
    step = pl.program_id(0)
    core = core_ref[0]
    att_ref = att_refs[0]
    for index, weight_refs in ((core, own_refs), (1 - core, other_refs)):
        part = step * 2 + index
        place = index * 4 + step
        resid = resid_ref[:, pl.ds(pl.multiple_of(part * CHUNK, CHUNK), CHUNK)]
        projected = resid.astype(jnp.float32)
        for y in range(4):
            weight = jnp.concatenate([weight_refs[y][0, z, :128, :] for z in range(4)], axis=0)
            projected = projected + jnp.dot(att_ref[y], weight, preferred_element_type=jnp.float32)
        hidden_ref[part] = projected
        for y in range(4):
            for z in range(4):
                extra = weight_refs[y][0, z, 128:, :]
                rows = jnp.concatenate([extra[:, :128], extra[:, 128:]], axis=0)
                head_ref[place, :, (z * 4 + y) * 128 : (z * 4 + y + 1) * 128] = rows

    @pl.when(step == 3)
    def _():
        count = hidden_ref.shape[1]
        squares = jnp.zeros((count, CHUNK), jnp.float32)
        for i in range(PARTS):
            squares = squares + hidden_ref[i] * hidden_ref[i]
        rinv = lax.rsqrt(jnp.sum(squares, axis=1, keepdims=True) / WIDTH + EPSILON)
        gains = []
        theta = jnp.zeros((PARTS * ROWS, count), jnp.float32)
        for i in range(PARTS):
            cols = slice(i * CHUNK, (i + 1) * CHUNK)
            gain = head_ref[0, :, cols].astype(jnp.float32)[REAL : REAL + 1, :]
            gains.append(gain)
            normed = (hidden_ref[i] * rinv * gain).astype(jnp.bfloat16)
            normed_ref[i] = normed
            head = head_ref[:, :, cols].reshape(PARTS * ROWS, CHUNK)
            theta = theta + lax.dot_general(head, normed, (((1,), (1,)), ((), ())), preferred_element_type=jnp.float32)
        for b in range(PARTS):
            theta_ref[b * REAL : (b + 1) * REAL, :] = theta[b * ROWS : b * ROWS + REAL, :]
        gap = goals_ref[...] - theta
        slope = jnp.abs(tau_ref[...] - jnp.where(gap < 0.0, 1.0, 0.0))
        dquant = -live_ref[...] * slope * jnp.clip(gap, -1.0, 1.0)
        dquant = jnp.where(real_ref[...] > 0.0, dquant, 0.0).astype(jnp.bfloat16)
        inner = jnp.zeros((count, CHUNK), jnp.float32)
        scaled = []
        row = lax.broadcasted_iota(jnp.int32, (PARTS * ROWS, CHUNK), 0)
        for i in range(PARTS):
            cols = slice(i * CHUNK, (i + 1) * CHUNK)
            head = head_ref[:, :, cols].reshape(PARTS * ROWS, CHUNK)
            dnormed = lax.dot_general(dquant, head, (((0,), (0,)), ((), ())), preferred_element_type=jnp.float32)
            product = dnormed * hidden_ref[i]
            inner = inner + product * gains[i]
            gain_term = jnp.sum(product * rinv, axis=0, keepdims=True)
            term = jnp.dot(dquant, normed_ref[i], preferred_element_type=jnp.float32)
            term = jnp.where(row == REAL, gain_term, term) * (1.0 / 8192)
            term = term.astype(jnp.bfloat16).reshape(2, 4, ROWS, CHUNK)
            for half in range(2):
                j = 2 * i + half
                share_ref[:, :, j % 4, j // 4] = term[:, :, :, half * 128 : (half + 1) * 128]
            scaled.append(dnormed * gains[i])
        mean = jnp.sum(inner, axis=1, keepdims=True) / WIDTH
        back = rinv * rinv * rinv * mean
        for i in range(PARTS):
            cols = slice(i * CHUNK, (i + 1) * CHUNK)
            token_ref[:, cols] = (rinv * scaled[i] - hidden_ref[i] * back).astype(jnp.bfloat16)


def head_pass(core, attended, own, other, resid, goals, live):
    rows = resid.shape[0]
    index = jnp.arange(PARTS * ROWS, dtype=jnp.int32)
    inside = index % ROWS
    tau = ((index // ROWS * REAL + inside).astype(jnp.float32) + 0.5) / QUANTILES
    real = (inside < REAL).astype(jnp.float32)
    whole = lambda shape: pl.BlockSpec(shape, lambda s, c: (0,) * len(shape))
    column = (PARTS * ROWS, 1)
    slot = lambda s, y, c: c * (s * 4 + y) + (1 - c) * (y * 4 + s)
    block = (1, 4, BLOCK, CHUNK)
    own_specs = [pl.BlockSpec(block, lambda s, c, y=y: (slot(s, y, c[0]), 0, 0, 0)) for y in range(4)]
    other_specs = [pl.BlockSpec(block, lambda s, c, y=y: (slot(s, y, 1 - c[0]), 0, 0, 0)) for y in range(4)]
    return pl.pallas_call(
        head_kernel,
        grid_spec=pltpu.PrefetchScalarGridSpec(
            num_scalar_prefetch=1,
            grid=(4,),
            in_specs=[whole(a.shape) for a in attended]
            + own_specs
            + other_specs
            + [whole((rows, WIDTH)), whole((1, rows)), whole((1, rows)), whole(column), whole(column)],
            out_specs=[whole((QUANTILES, rows)), whole((rows, WIDTH)), whole((2, 4, 4, 4, ROWS, 128))],
            scratch_shapes=[
                pltpu.VMEM((PARTS, rows, CHUNK), jnp.float32),
                pltpu.VMEM((PARTS, ROWS, WIDTH), jnp.bfloat16),
                pltpu.VMEM((PARTS, rows, CHUNK), jnp.bfloat16),
            ],
        ),
        out_shape=[
            jax.ShapeDtypeStruct((QUANTILES, rows), jnp.float32),
            jax.ShapeDtypeStruct((rows, WIDTH), jnp.bfloat16),
            jax.ShapeDtypeStruct((2, 4, 4, 4, ROWS, 128), jnp.bfloat16),
        ],
        compiler_params=pltpu.CompilerParams(vmem_limit_bytes=26 * 2**20),
        cost_estimate=pl.CostEstimate(flops=3 * 10**9, bytes_accessed=13 * 2**20, transcendentals=0),
    )(core[None], *attended, *[own] * 4, *[other] * 4, resid, goals, live, tau[:, None], real[:, None])


def exchange(value, axes):
    return lax.all_to_all(value, axes, 0, 0, tiled=False)


def plane_groups(mixed):
    place = lambda x, h, c, z, y: (((x * 4 + h) * 2 + c) * 4 + z) * 4 + y
    groups = []
    for h in range(4):
        for c in range(2):
            for z in range(4):
                for i in range(4):
                    if (c == 0) == mixed:
                        groups.append([place(k, h, c, z, i) for k in range(4)])
                    else:
                        groups.append([place(i, h, c, z, k) for k in range(4)])
    return groups


def spread(value, first):
    copies = jnp.broadcast_to(value[None], (4,) + value.shape)
    return lax.all_to_all(copies, AXES, 0, 0, axis_index_groups=plane_groups(first), tiled=False)


def ring(value, axes, count, steps):
    return lax.ppermute(value, axes, [(i, (i + steps) % count) for i in range(count)])


def total(pieces):
    return jnp.sum(pieces.astype(jnp.float32), axis=0)


def gather_weights(out_weight, head_weight, gain, packed_kv, ready):
    x, core = lax.axis_index("x"), lax.axis_index("core")
    columns = lax.dynamic_slice_in_dim(out_weight, (x * 2 + core) * CHUNK, CHUNK, axis=1)
    block = core * 4 + x
    head_rows = lax.dynamic_slice_in_dim(head_weight.T, block * REAL, REAL, axis=0)
    gain_row = jnp.where(block == 0, gain, jnp.zeros_like(gain))[None, :]
    rest = jnp.zeros((ROWS - REAL - 1, 128), jnp.bfloat16)
    packed = jnp.concatenate([head_rows, gain_row, rest], axis=0)
    packed = jnp.concatenate([packed[:16], packed[16:]], axis=1)
    mine = jnp.concatenate([columns, packed], axis=0)
    def passed(piece):
        return spread(spread(piece, True), False).reshape(16, 4, BLOCK, CHUNK)

    along_z = exchange(jnp.broadcast_to(mine[None], (4,) + mine.shape), "zl")
    along_z, packed_kv, ready = lax.optimization_barrier((along_z, packed_kv, ready))
    far = ring(packed_kv, ("x", "zh"), 16, 1)
    own = lax.cond(ready, passed, lambda piece: jnp.zeros((16, 4, BLOCK, CHUNK), jnp.bfloat16), along_z)
    return lax.optimization_barrier((own, far))


def reduce_shares(share):
    both = total(exchange(share, "core")).astype(jnp.bfloat16)
    plane = total(exchange(both.reshape(16, 4, ROWS, 128), ("x", "y"))).astype(jnp.bfloat16)
    spread = jnp.broadcast_to(plane[None], (4, 4, ROWS, 128)).reshape(16, ROWS, 128)
    line = total(exchange(spread, ("zh", "zl"))).astype(jnp.bfloat16)
    parts = exchange(jnp.broadcast_to(line[None], (PARTS, ROWS, 128)), ("x", "core"))
    parts = parts.reshape(4, 2, ROWS, 128).transpose(1, 0, 2, 3).astype(jnp.float32)
    grad_head = parts[:, :, :REAL].reshape(QUANTILES, 128).T
    return grad_head, parts[0, 0, REAL]


def local(queries, keys, values, resid, out_weight, head_weight, gain, doc_ids, prompt_lengths, targets):
    rows = queries.shape[1]
    core = lax.axis_index("core")
    place = (lax.axis_index("x") * 4 + lax.axis_index("zh")) * 2 + core
    own = jnp.concatenate([keys[0], values[0]], axis=1)
    mine, far = gather_weights(out_weight, head_weight, gain, own, doc_ids[0, 0] >= 0)
    near = ring(jnp.where(core == 0, own, far), "core", 2, 1)
    mine, near = lax.optimization_barrier((mine, near))
    other = ring(mine, "core", 2, 1)

    ids = doc_ids[0]
    first = place * rows
    query_ids = lax.dynamic_slice_in_dim(ids, first, rows)
    docs = jnp.arange(prompt_lengths.shape[1], dtype=jnp.int32)
    starts = jnp.sum((ids[None, :] < docs[:, None]).astype(jnp.int32), axis=1)
    onehot = (query_ids[:, None] == docs[None, :]).astype(jnp.int32)
    own_start = jnp.sum(onehot * starts[None, :], axis=1)
    own_prompt = jnp.sum(onehot * prompt_lengths[0][None, :], axis=1)
    query_pos = first + jnp.arange(rows, dtype=jnp.int32)
    live = (query_pos - own_start >= own_prompt).astype(jnp.float32)
    key_pos = first - SPAN * rows + jnp.arange((SPAN + 1) * rows, dtype=jnp.int32)
    allowed = (key_pos[None, :] >= own_start[:, None]) & (key_pos[None, :] <= query_pos[:, None])
    bias = jnp.where(allowed, 0.0, NEGATIVE).astype(jnp.float32)

    attended = [attend(queries[0], 0, own, near, far, bias)]
    theta, token_grad, share = head_pass(core, attended, mine, other, resid[0], targets, live[None, :])
    grad_head, grad_gain = reduce_shares(share)
    return theta.T[None], token_grad[None], grad_head, grad_gain


def solution(mesh):
    fine = Mesh(mesh.devices.reshape(EXTENT), AXES)
    ctx, dp = ("x", "zh", "core"), ("zl", "y")
    in_specs = (
        P(dp, ctx, None),
        P(dp, ctx, None),
        P(dp, ctx, None),
        P(dp, ctx, None),
        P(dp, None),
        P(dp, None),
        P(dp),
        P(dp, None),
        P(dp, None),
        P(dp, ctx),
    )
    out_specs = (P(dp, ctx, None), P(dp, ctx, None), P(dp, None), P(dp))
    return jax.shard_map(local, mesh=fine, in_specs=in_specs, out_specs=out_specs, check_vma=False)
```

```python
import math

import jax
import jax.numpy as jnp
from jax import lax
from jax.experimental import pallas as pl
from jax.experimental.pallas import tpu as pltpu
from jax.sharding import Mesh, PartitionSpec as P

AXES = ("x", "zh", "core", "zl", "y")
EXTENT = (4, 4, 2, 4, 4)
QUERY_HEADS = 16
KV_HEADS = 4
HEAD_SIZE = 128
SPAN = 2
WIDTH = 2048
QUANTILES = 200
EPSILON = 1e-05
NEGATIVE = -1e30
PARTS = 8
REAL = QUANTILES // PARTS
ROWS = 32
CHUNK = WIDTH // PARTS
BLOCK = 128 + 16
ATTEND_COST = 18 * 10**9


def attend_kernel(q_ref, k0_ref, k1_ref, k2_ref, v0_ref, v1_ref, v2_ref, bias_ref, out_ref):
    keys = jnp.concatenate([k0_ref[...], k1_ref[...], k2_ref[...]], axis=0)
    values = jnp.concatenate([v0_ref[...], v1_ref[...], v2_ref[...]], axis=0)
    values = jnp.concatenate([values, jnp.ones(values.shape, values.dtype)], axis=1)
    factor = HEAD_SIZE**-0.5 * math.log2(math.e)
    members = QUERY_HEADS // KV_HEADS
    rows = q_ref.shape[0] // 2
    reach = keys.shape[0] - rows
    jobs = [(m, h * rows) for m in range(members) for h in range(2)]
    scores = []
    for member, row in jobs:
        q = q_ref[row : row + rows, member * HEAD_SIZE : (member + 1) * HEAD_SIZE]
        product = lax.dot_general(q, keys[row : row + reach], (((1,), (1,)), ((), ())), preferred_element_type=jnp.float32)
        scores.append(product + bias_ref[row : row + rows, row : row + reach])
    weights = [jnp.exp2((s - jnp.max(s, axis=1, keepdims=True)) * factor).astype(jnp.bfloat16) for s in scores]
    for (member, row), weight in zip(jobs, weights):
        mixed = jnp.dot(weight, values[row : row + reach], preferred_element_type=jnp.float32)
        mixed = mixed[:, :HEAD_SIZE] / mixed[:, HEAD_SIZE:]
        out_ref[member, row : row + rows] = mixed.astype(jnp.bfloat16)


def attend(queries, first, own, near, far, bias):
    rows = queries.shape[0]
    heads = own.shape[1] // (2 * HEAD_SIZE)
    one = (rows, HEAD_SIZE)
    key_spec = pl.BlockSpec(one, lambda g: (0, g))
    value_spec = pl.BlockSpec(one, lambda g: (0, g + heads))
    return pl.pallas_call(
        attend_kernel,
        grid=(heads,),
        in_specs=[pl.BlockSpec((rows, 4 * HEAD_SIZE), lambda g: (0, g + first))]
        + [key_spec] * 3
        + [value_spec] * 3
        + [pl.BlockSpec(bias.shape, lambda g: (0, 0))],
        out_specs=pl.BlockSpec((4, rows, HEAD_SIZE), lambda g: (0, 0, g)),
        out_shape=jax.ShapeDtypeStruct((4, rows, heads * HEAD_SIZE), jnp.bfloat16),
        compiler_params=pltpu.CompilerParams(vmem_limit_bytes=16 * 2**20),
        cost_estimate=pl.CostEstimate(
            flops=ATTEND_COST, bytes_accessed=heads * 2**20, transcendentals=4 * heads * 256 * 768
        ),
    )(queries, far, near, own, far, near, own, bias)


def project_kernel(core_ref, own_ref, other_ref, *refs):
    weight_refs, (near_ref, send_ref) = refs[:4], refs[4:]
    rows = own_ref.shape[1]
    total = None
    for y in range(4):
        weight = jnp.concatenate([weight_refs[y][0, z, :128, :] for z in range(4)], axis=0)
        both = jnp.concatenate([own_ref[y], other_ref[y]], axis=0)
        part = jnp.dot(both, weight, preferred_element_type=jnp.float32)
        total = part if total is None else total + part
        for z in range(4):
            extra = weight_refs[y][0, z, 128:, :]
            block = jnp.concatenate([extra[:, :128], extra[:, 128:]], axis=0)
            i, half = divmod(z * 4 + y, 2)
            send_ref[1, 0, i * ROWS : (i + 1) * ROWS, half * 128 : (half + 1) * 128] = block
    near_ref[0] = total[:rows]
    send_ref[0, 0] = total[rows:].astype(jnp.bfloat16)


def project(core, attended, other, plane):
    rows = attended.shape[1]
    slot = lambda s, y, c: c * (s * 4 + y) + (1 - c) * (y * 4 + s)
    block = (1, 4, BLOCK, CHUNK)
    weight_specs = [pl.BlockSpec(block, lambda s, c, y=y: (slot(s, y, c[0]), 0, 0, 0)) for y in range(4)]
    whole = lambda a: pl.BlockSpec(a.shape, lambda s, c: (0,) * a.ndim)
    return pl.pallas_call(
        project_kernel,
        grid_spec=pltpu.PrefetchScalarGridSpec(
            num_scalar_prefetch=1,
            grid=(4,),
            in_specs=[whole(attended), whole(other)] + weight_specs,
            out_specs=[
                pl.BlockSpec((1, rows, CHUNK), lambda s, c: (s, 0, 0)),
                pl.BlockSpec((2, 1, rows, CHUNK), lambda s, c: (0, s, 0, 0)),
            ],
        ),
        out_shape=[
            jax.ShapeDtypeStruct((4, rows, CHUNK), jnp.float32),
            jax.ShapeDtypeStruct((2, 4, rows, CHUNK), jnp.bfloat16),
        ],
        compiler_params=pltpu.CompilerParams(vmem_limit_bytes=20 * 2**20),
        cost_estimate=pl.CostEstimate(flops=2 * 10**9, bytes_accessed=7 * 2**20, transcendentals=0),
    )(core[None], attended, other, *[plane] * 4)


def head_kernel(
    core_ref, near_ref, sent_ref, received_ref, resid_ref, goals_ref, live_ref, tau_ref, real_ref,
    theta_ref, token_ref, share_ref, hidden_ref, head_ref, normed_ref,
):
    core = core_ref[0]
    for x in range(4):
        for index, projected in ((core, near_ref[x]), (1 - core, received_ref[0, x].astype(jnp.float32))):
            part = x * 2 + index
            resid = resid_ref[:, pl.ds(pl.multiple_of(part * CHUNK, CHUNK), CHUNK)]
            hidden_ref[part] = projected + resid.astype(jnp.float32)
        for i in range(PARTS):
            cols = slice(i * CHUNK, (i + 1) * CHUNK)
            head_ref[core * 4 + x, :, cols] = sent_ref[1, x, i * ROWS : (i + 1) * ROWS, :]
            head_ref[(1 - core) * 4 + x, :, cols] = received_ref[1, x, i * ROWS : (i + 1) * ROWS, :]

    count = hidden_ref.shape[1]
    squares = jnp.zeros((count, CHUNK), jnp.float32)
    for i in range(PARTS):
        squares = squares + hidden_ref[i] * hidden_ref[i]
    rinv = lax.rsqrt(jnp.sum(squares, axis=1, keepdims=True) / WIDTH + EPSILON)
    gains = []
    theta = jnp.zeros((PARTS * ROWS, count), jnp.float32)
    for i in range(PARTS):
        cols = slice(i * CHUNK, (i + 1) * CHUNK)
        gain = head_ref[0, :, cols].astype(jnp.float32)[REAL : REAL + 1, :]
        gains.append(gain)
        normed = (hidden_ref[i] * rinv * gain).astype(jnp.bfloat16)
        normed_ref[i] = normed
        head = head_ref[:, :, cols].reshape(PARTS * ROWS, CHUNK)
        theta = theta + lax.dot_general(head, normed, (((1,), (1,)), ((), ())), preferred_element_type=jnp.float32)
    for b in range(PARTS):
        theta_ref[b * REAL : (b + 1) * REAL, :] = theta[b * ROWS : b * ROWS + REAL, :]
    gap = goals_ref[...] - theta
    slope = jnp.abs(tau_ref[...] - jnp.where(gap < 0.0, 1.0, 0.0))
    dquant = -live_ref[...] * slope * jnp.clip(gap, -1.0, 1.0)
    dquant = jnp.where(real_ref[...] > 0.0, dquant, 0.0).astype(jnp.bfloat16)
    inner = jnp.zeros((count, CHUNK), jnp.float32)
    scaled = []
    row = lax.broadcasted_iota(jnp.int32, (PARTS * ROWS, CHUNK), 0)
    for i in range(PARTS):
        cols = slice(i * CHUNK, (i + 1) * CHUNK)
        head = head_ref[:, :, cols].reshape(PARTS * ROWS, CHUNK)
        dnormed = lax.dot_general(dquant, head, (((0,), (0,)), ((), ())), preferred_element_type=jnp.float32)
        product = dnormed * hidden_ref[i]
        inner = inner + product * gains[i]
        gain_term = jnp.sum(product * rinv, axis=0, keepdims=True)
        term = jnp.dot(dquant, normed_ref[i], preferred_element_type=jnp.float32)
        term = jnp.where(row == REAL, gain_term, term) * (1.0 / 8192)
        term = term.astype(jnp.bfloat16).reshape(2, 4, ROWS, CHUNK)
        for half in range(2):
            j = 2 * i + half
            share_ref[:, :, j % 4, j // 4] = term[:, :, :, half * 128 : (half + 1) * 128]
        scaled.append(dnormed * gains[i])
    mean = jnp.sum(inner, axis=1, keepdims=True) / WIDTH
    back = rinv * rinv * rinv * mean
    for i in range(PARTS):
        cols = slice(i * CHUNK, (i + 1) * CHUNK)
        token_ref[:, cols] = (rinv * scaled[i] - hidden_ref[i] * back).astype(jnp.bfloat16)


def head_pass(core, near, sent, received, resid, goals, live):
    rows = resid.shape[0]
    index = jnp.arange(PARTS * ROWS, dtype=jnp.int32)
    inside = index % ROWS
    tau = ((index // ROWS * REAL + inside).astype(jnp.float32) + 0.5) / QUANTILES
    real = (inside < REAL).astype(jnp.float32)
    vmem = pl.BlockSpec(memory_space=pltpu.VMEM)
    return pl.pallas_call(
        head_kernel,
        in_specs=[pl.BlockSpec(memory_space=pltpu.SMEM)] + [vmem] * 8,
        out_specs=[vmem] * 3,
        out_shape=[
            jax.ShapeDtypeStruct((QUANTILES, rows), jnp.float32),
            jax.ShapeDtypeStruct((rows, WIDTH), jnp.bfloat16),
            jax.ShapeDtypeStruct((2, 4, 4, 4, ROWS, 128), jnp.bfloat16),
        ],
        scratch_shapes=[
            pltpu.VMEM((PARTS, rows, CHUNK), jnp.float32),
            pltpu.VMEM((PARTS, ROWS, WIDTH), jnp.bfloat16),
            pltpu.VMEM((PARTS, rows, CHUNK), jnp.bfloat16),
        ],
        compiler_params=pltpu.CompilerParams(vmem_limit_bytes=26 * 2**20),
        cost_estimate=pl.CostEstimate(flops=10**9, bytes_accessed=8 * 2**20, transcendentals=0),
    )(core[None], near, sent, received, resid, goals, live, tau[:, None], real[:, None])


def exchange(value, axes):
    return lax.all_to_all(value, axes, 0, 0, tiled=False)


def plane_groups(mixed):
    place = lambda x, h, c, z, y: (((x * 4 + h) * 2 + c) * 4 + z) * 4 + y
    groups = []
    for h in range(4):
        for c in range(2):
            for z in range(4):
                for i in range(4):
                    if (c == 0) == mixed:
                        groups.append([place(k, h, c, z, i) for k in range(4)])
                    else:
                        groups.append([place(i, h, c, z, k) for k in range(4)])
    return groups


def copy_kernel(value_ref, out_ref, sems):
    copies = [pltpu.make_async_copy(value_ref, out_ref.at[i], sems.at[i]) for i in range(4)]
    for copy in copies:
        copy.start()
    for copy in copies:
        copy.wait()


def four_copies(value):
    return pl.pallas_call(
        copy_kernel,
        in_specs=[pl.BlockSpec(memory_space=pltpu.VMEM)],
        out_specs=pl.BlockSpec(memory_space=pl.ANY),
        out_shape=jax.ShapeDtypeStruct((4,) + value.shape, value.dtype),
        scratch_shapes=[pltpu.SemaphoreType.DMA((4,))],
        cost_estimate=pl.CostEstimate(flops=0, bytes_accessed=5 * value.size * 2, transcendentals=0),
    )(value)


def spread(value, first):
    copies = jnp.broadcast_to(value[None], (4,) + value.shape) if first else four_copies(value)
    return lax.all_to_all(copies, AXES, 0, 0, axis_index_groups=plane_groups(first), tiled=False)


def ring(value, axes, count, steps):
    return lax.ppermute(value, axes, [(i, (i + steps) % count) for i in range(count)])


def total(pieces):
    return jnp.sum(pieces.astype(jnp.float32), axis=0)


def gather_z(out_weight, head_weight, gain):
    x, core = lax.axis_index("x"), lax.axis_index("core")
    columns = lax.dynamic_slice_in_dim(out_weight, (x * 2 + core) * CHUNK, CHUNK, axis=1)
    block = core * 4 + x
    head_rows = lax.dynamic_slice_in_dim(head_weight.T, block * REAL, REAL, axis=0)
    gain_row = jnp.where(block == 0, gain, jnp.zeros_like(gain))[None, :]
    rest = jnp.zeros((ROWS - REAL - 1, 128), jnp.bfloat16)
    packed = jnp.concatenate([head_rows, gain_row, rest], axis=0)
    packed = jnp.concatenate([packed[:16], packed[16:]], axis=1)
    mine = jnp.concatenate([columns, packed], axis=0)
    two = jnp.stack([mine, ring(mine, ("zh", "zl"), 16, -1)])
    return two, ring(two, ("zh", "zl"), 16, -2)


def first_spread(*slots):
    slots = jnp.concatenate(slots + slots)
    along_z = lax.dynamic_slice_in_dim(slots, (4 - lax.axis_index("zl")) % 4, 4, axis=0)
    return spread(along_z, True)


def reduce_shares(share):
    both = total(exchange(share, "core")).astype(jnp.bfloat16)
    plane = total(exchange(both.reshape(16, 4, ROWS, 128), ("x", "y"))).astype(jnp.bfloat16)
    spread = jnp.broadcast_to(plane[None], (4, 4, ROWS, 128)).reshape(16, ROWS, 128)
    line = total(exchange(spread, ("zh", "zl"))).astype(jnp.bfloat16)
    parts = exchange(jnp.broadcast_to(line[None], (PARTS, ROWS, 128)), ("x", "core"))
    parts = parts.reshape(4, 2, ROWS, 128).transpose(1, 0, 2, 3).astype(jnp.float32)
    grad_head = parts[:, :, :REAL].reshape(QUANTILES, 128).T
    return grad_head, parts[0, 0, REAL]


def local(queries, keys, values, resid, out_weight, head_weight, gain, doc_ids, prompt_lengths, targets):
    rows = queries.shape[1]
    core = lax.axis_index("core")
    place = (lax.axis_index("x") * 4 + lax.axis_index("zh")) * 2 + core
    own = jnp.concatenate([keys[0], values[0]], axis=1)
    far = ring(own, ("x", "zh"), 16, 1)
    slots = gather_z(out_weight, head_weight, gain)
    lines = lax.cond(place >= 0, first_spread, lambda *s: jnp.zeros((4, 4, BLOCK, CHUNK), jnp.bfloat16), *slots)
    plane = spread(lines, False).reshape(16, 4, BLOCK, CHUNK)
    near = ring(jnp.where(core == 0, own, far), "core", 2, 1)

    ids = doc_ids[0]
    first = place * rows
    query_ids = lax.dynamic_slice_in_dim(ids, first, rows)
    docs = jnp.arange(prompt_lengths.shape[1], dtype=jnp.int32)
    starts = jnp.sum((ids[None, :] < docs[:, None]).astype(jnp.int32), axis=1)
    onehot = (query_ids[:, None] == docs[None, :]).astype(jnp.int32)
    own_start = jnp.sum(onehot * starts[None, :], axis=1)
    own_prompt = jnp.sum(onehot * prompt_lengths[0][None, :], axis=1)
    query_pos = first + jnp.arange(rows, dtype=jnp.int32)
    live = (query_pos - own_start >= own_prompt).astype(jnp.float32)
    key_pos = first - SPAN * rows + jnp.arange((SPAN + 1) * rows, dtype=jnp.int32)
    allowed = (key_pos[None, :] >= own_start[:, None]) & (key_pos[None, :] <= query_pos[:, None])
    bias = jnp.where(allowed, 0.0, NEGATIVE).astype(jnp.float32)

    attended = attend(queries[0], 0, own, near, far, bias)
    kept, sent = project(core, attended, ring(attended, "core", 2, 1), plane)
    theta, token_grad, share = head_pass(core, kept, sent, ring(sent, "core", 2, 1), resid[0], targets, live[None, :])
    grad_head, grad_gain = reduce_shares(share)
    return theta.T[None], token_grad[None], grad_head, grad_gain


def solution(mesh):
    fine = Mesh(mesh.devices.reshape(EXTENT), AXES)
    ctx, dp = ("x", "zh", "core"), ("zl", "y")
    in_specs = (
        P(dp, ctx, None),
        P(dp, ctx, None),
        P(dp, ctx, None),
        P(dp, ctx, None),
        P(dp, None),
        P(dp, None),
        P(dp),
        P(dp, None),
        P(dp, None),
        P(dp, ctx),
    )
    out_specs = (P(dp, ctx, None), P(dp, ctx, None), P(dp, None), P(dp))
    return jax.shard_map(local, mesh=fine, in_specs=in_specs, out_specs=out_specs, check_vma=False)
```

```python
import math

import jax
import jax.numpy as jnp
from jax import lax
from jax.experimental import pallas as pl
from jax.experimental.pallas import tpu as pltpu
from jax.sharding import Mesh, PartitionSpec as P

AXES = ("x", "zh", "core", "zl", "y")
EXTENT = (4, 4, 2, 4, 4)
QUERY_HEADS = 16
KV_HEADS = 4
HEAD_SIZE = 128
SPAN = 2
WIDTH = 2048
QUANTILES = 200
EPSILON = 1e-05
NEGATIVE = -1e30
PARTS = 8
REAL = QUANTILES // PARTS
ROWS = 32
CHUNK = WIDTH // PARTS
BLOCK = 128 + 16
ATTEND_COST = 18 * 10**9


def attend_kernel(q_ref, k0_ref, k1_ref, k2_ref, v0_ref, v1_ref, v2_ref, bias_ref, out_ref):
    keys = jnp.concatenate([k0_ref[...], k1_ref[...], k2_ref[...]], axis=0)
    values = jnp.concatenate([v0_ref[...], v1_ref[...], v2_ref[...]], axis=0)
    values = jnp.concatenate([values, jnp.ones(values.shape, values.dtype)], axis=1)
    factor = HEAD_SIZE**-0.5 * math.log2(math.e)
    members = QUERY_HEADS // KV_HEADS
    rows = q_ref.shape[0] // 2
    reach = keys.shape[0] - rows
    jobs = [(m, h * rows) for m in range(members) for h in range(2)]
    scores = []
    for member, row in jobs:
        q = q_ref[row : row + rows, member * HEAD_SIZE : (member + 1) * HEAD_SIZE]
        product = lax.dot_general(q, keys[row : row + reach], (((1,), (1,)), ((), ())), preferred_element_type=jnp.float32)
        scores.append(product + bias_ref[row : row + rows, row : row + reach])
    weights = [jnp.exp2((s - jnp.max(s, axis=1, keepdims=True)) * factor).astype(jnp.bfloat16) for s in scores]
    for (member, row), weight in zip(jobs, weights):
        mixed = jnp.dot(weight, values[row : row + reach], preferred_element_type=jnp.float32)
        mixed = mixed[:, :HEAD_SIZE] / mixed[:, HEAD_SIZE:]
        out_ref[member, row : row + rows] = mixed.astype(jnp.bfloat16)


def attend(queries, first, own, near, far, bias):
    rows = queries.shape[0]
    heads = own.shape[1] // (2 * HEAD_SIZE)
    one = (rows, HEAD_SIZE)
    key_spec = pl.BlockSpec(one, lambda g: (0, g))
    value_spec = pl.BlockSpec(one, lambda g: (0, g + heads))
    return pl.pallas_call(
        attend_kernel,
        grid=(heads,),
        in_specs=[pl.BlockSpec((rows, 4 * HEAD_SIZE), lambda g: (0, g + first))]
        + [key_spec] * 3
        + [value_spec] * 3
        + [pl.BlockSpec(bias.shape, lambda g: (0, 0))],
        out_specs=pl.BlockSpec((4, rows, HEAD_SIZE), lambda g: (0, 0, g)),
        out_shape=jax.ShapeDtypeStruct((4, rows, heads * HEAD_SIZE), jnp.bfloat16),
        compiler_params=pltpu.CompilerParams(vmem_limit_bytes=16 * 2**20),
        cost_estimate=pl.CostEstimate(
            flops=ATTEND_COST, bytes_accessed=heads * 2**20, transcendentals=4 * heads * 256 * 768
        ),
    )(queries, far, near, own, far, near, own, bias)


def project_kernel(core_ref, own_ref, other_ref, *refs):
    weight_refs, (near_ref, send_ref) = refs[:4], refs[4:]
    rows = own_ref.shape[1]
    total = None
    for y in range(4):
        weight = jnp.concatenate([weight_refs[y][0, z, :128, :] for z in range(4)], axis=0)
        both = jnp.concatenate([own_ref[y], other_ref[y]], axis=0)
        part = jnp.dot(both, weight, preferred_element_type=jnp.float32)
        total = part if total is None else total + part
        for z in range(4):
            extra = weight_refs[y][0, z, 128:, :]
            block = jnp.concatenate([extra[:, :128], extra[:, 128:]], axis=0)
            i, half = divmod(z * 4 + y, 2)
            send_ref[1, 0, i * ROWS : (i + 1) * ROWS, half * 128 : (half + 1) * 128] = block
    near_ref[0] = total[:rows]
    send_ref[0, 0] = total[rows:].astype(jnp.bfloat16)


def project(core, attended, other, plane):
    rows = attended.shape[1]
    slot = lambda s, y, c: c * (s * 4 + y) + (1 - c) * (y * 4 + s)
    block = (1, 4, BLOCK, CHUNK)
    weight_specs = [pl.BlockSpec(block, lambda s, c, y=y: (slot(s, y, c[0]), 0, 0, 0)) for y in range(4)]
    whole = lambda a: pl.BlockSpec(a.shape, lambda s, c: (0,) * a.ndim)
    return pl.pallas_call(
        project_kernel,
        grid_spec=pltpu.PrefetchScalarGridSpec(
            num_scalar_prefetch=1,
            grid=(4,),
            in_specs=[whole(attended), whole(other)] + weight_specs,
            out_specs=[
                pl.BlockSpec((1, rows, CHUNK), lambda s, c: (s, 0, 0)),
                pl.BlockSpec((2, 1, rows, CHUNK), lambda s, c: (0, s, 0, 0)),
            ],
        ),
        out_shape=[
            jax.ShapeDtypeStruct((4, rows, CHUNK), jnp.float32),
            jax.ShapeDtypeStruct((2, 4, rows, CHUNK), jnp.bfloat16),
        ],
        compiler_params=pltpu.CompilerParams(vmem_limit_bytes=20 * 2**20),
        cost_estimate=pl.CostEstimate(flops=2 * 10**9, bytes_accessed=7 * 2**20, transcendentals=0),
    )(core[None], attended, other, *[plane] * 4)


def head_kernel(
    core_ref, near_ref, sent_ref, received_ref, resid_ref, goals_ref, live_ref, tau_ref, real_ref,
    theta_ref, token_ref, share_ref, hidden_ref, head_ref, normed_ref,
):
    core = core_ref[0]
    for x in range(4):
        for index, projected in ((core, near_ref[x]), (1 - core, received_ref[0, x].astype(jnp.float32))):
            part = x * 2 + index
            resid = resid_ref[:, pl.ds(pl.multiple_of(part * CHUNK, CHUNK), CHUNK)]
            hidden_ref[part] = projected + resid.astype(jnp.float32)
        for i in range(PARTS):
            cols = slice(i * CHUNK, (i + 1) * CHUNK)
            head_ref[core * 4 + x, :, cols] = sent_ref[1, x, i * ROWS : (i + 1) * ROWS, :]
            head_ref[(1 - core) * 4 + x, :, cols] = received_ref[1, x, i * ROWS : (i + 1) * ROWS, :]

    count = hidden_ref.shape[1]
    squares = jnp.zeros((count, CHUNK), jnp.float32)
    for i in range(PARTS):
        squares = squares + hidden_ref[i] * hidden_ref[i]
    rinv = lax.rsqrt(jnp.sum(squares, axis=1, keepdims=True) / WIDTH + EPSILON)
    gains = []
    theta = jnp.zeros((PARTS * ROWS, count), jnp.float32)
    for i in range(PARTS):
        cols = slice(i * CHUNK, (i + 1) * CHUNK)
        gain = head_ref[0, :, cols].astype(jnp.float32)[REAL : REAL + 1, :]
        gains.append(gain)
        normed = (hidden_ref[i] * rinv * gain).astype(jnp.bfloat16)
        normed_ref[i] = normed
        head = head_ref[:, :, cols].reshape(PARTS * ROWS, CHUNK)
        theta = theta + lax.dot_general(head, normed, (((1,), (1,)), ((), ())), preferred_element_type=jnp.float32)
    for b in range(PARTS):
        theta_ref[b * REAL : (b + 1) * REAL, :] = theta[b * ROWS : b * ROWS + REAL, :]
    gap = goals_ref[...] - theta
    slope = jnp.abs(tau_ref[...] - jnp.where(gap < 0.0, 1.0, 0.0))
    dquant = -live_ref[...] * slope * jnp.clip(gap, -1.0, 1.0)
    dquant = jnp.where(real_ref[...] > 0.0, dquant, 0.0).astype(jnp.bfloat16)
    inner = jnp.zeros((count, CHUNK), jnp.float32)
    scaled = []
    row = lax.broadcasted_iota(jnp.int32, (PARTS * ROWS, CHUNK), 0)
    for i in range(PARTS):
        cols = slice(i * CHUNK, (i + 1) * CHUNK)
        head = head_ref[:, :, cols].reshape(PARTS * ROWS, CHUNK)
        dnormed = lax.dot_general(dquant, head, (((0,), (0,)), ((), ())), preferred_element_type=jnp.float32)
        product = dnormed * hidden_ref[i]
        inner = inner + product * gains[i]
        gain_term = jnp.sum(product * rinv, axis=0, keepdims=True)
        term = jnp.dot(dquant, normed_ref[i], preferred_element_type=jnp.float32)
        term = jnp.where(row == REAL, gain_term, term) * (1.0 / 8192)
        term = term.astype(jnp.bfloat16).reshape(2, 4, ROWS, CHUNK)
        for half in range(2):
            j = 2 * i + half
            share_ref[:, :, j % 4, j // 4] = term[:, :, :, half * 128 : (half + 1) * 128]
        scaled.append(dnormed * gains[i])
    mean = jnp.sum(inner, axis=1, keepdims=True) / WIDTH
    back = rinv * rinv * rinv * mean
    for i in range(PARTS):
        cols = slice(i * CHUNK, (i + 1) * CHUNK)
        token_ref[:, cols] = (rinv * scaled[i] - hidden_ref[i] * back).astype(jnp.bfloat16)


def head_pass(core, near, sent, received, resid, goals, live):
    rows = resid.shape[0]
    index = jnp.arange(PARTS * ROWS, dtype=jnp.int32)
    inside = index % ROWS
    tau = ((index // ROWS * REAL + inside).astype(jnp.float32) + 0.5) / QUANTILES
    real = (inside < REAL).astype(jnp.float32)
    vmem = pl.BlockSpec(memory_space=pltpu.VMEM)
    return pl.pallas_call(
        head_kernel,
        in_specs=[pl.BlockSpec(memory_space=pltpu.SMEM)] + [vmem] * 8,
        out_specs=[vmem] * 3,
        out_shape=[
            jax.ShapeDtypeStruct((QUANTILES, rows), jnp.float32),
            jax.ShapeDtypeStruct((rows, WIDTH), jnp.bfloat16),
            jax.ShapeDtypeStruct((2, 4, 4, 4, ROWS, 128), jnp.bfloat16),
        ],
        scratch_shapes=[
            pltpu.VMEM((PARTS, rows, CHUNK), jnp.float32),
            pltpu.VMEM((PARTS, ROWS, WIDTH), jnp.bfloat16),
            pltpu.VMEM((PARTS, rows, CHUNK), jnp.bfloat16),
        ],
        compiler_params=pltpu.CompilerParams(vmem_limit_bytes=26 * 2**20),
        cost_estimate=pl.CostEstimate(flops=10**9, bytes_accessed=8 * 2**20, transcendentals=0),
    )(core[None], near, sent, received, resid, goals, live, tau[:, None], real[:, None])


def exchange(value, axes):
    return lax.all_to_all(value, axes, 0, 0, tiled=False)


def plane_groups(mixed):
    place = lambda x, h, c, z, y: (((x * 4 + h) * 2 + c) * 4 + z) * 4 + y
    groups = []
    for h in range(4):
        for c in range(2):
            for z in range(4):
                for i in range(4):
                    if (c == 0) == mixed:
                        groups.append([place(k, h, c, z, i) for k in range(4)])
                    else:
                        groups.append([place(i, h, c, z, k) for k in range(4)])
    return groups


def copy_kernel(value_ref, out_ref, sems):
    copies = [pltpu.make_async_copy(value_ref, out_ref.at[i], sems.at[i]) for i in range(4)]
    for copy in copies:
        copy.start()
    for copy in copies:
        copy.wait()


def four_copies(value):
    return pl.pallas_call(
        copy_kernel,
        in_specs=[pl.BlockSpec(memory_space=pltpu.VMEM)],
        out_specs=pl.BlockSpec(memory_space=pl.ANY),
        out_shape=jax.ShapeDtypeStruct((4,) + value.shape, value.dtype),
        scratch_shapes=[pltpu.SemaphoreType.DMA((4,))],
        cost_estimate=pl.CostEstimate(flops=0, bytes_accessed=5 * value.size * 2, transcendentals=0),
    )(value)


def spread(value, first):
    copies = jnp.broadcast_to(value[None], (4,) + value.shape) if first else four_copies(value)
    return lax.all_to_all(copies, AXES, 0, 0, axis_index_groups=plane_groups(first), tiled=False)


def ring(value, axes, count, steps):
    return lax.ppermute(value, axes, [(i, (i + steps) % count) for i in range(count)])


def total(pieces):
    return jnp.sum(pieces.astype(jnp.float32), axis=0)


def gather_z(out_weight, head_weight, gain):
    x, core = lax.axis_index("x"), lax.axis_index("core")
    columns = lax.dynamic_slice_in_dim(out_weight, (x * 2 + core) * CHUNK, CHUNK, axis=1)
    block = core * 4 + x
    head_rows = lax.dynamic_slice_in_dim(head_weight.T, block * REAL, REAL, axis=0)
    gain_row = jnp.where(block == 0, gain, jnp.zeros_like(gain))[None, :]
    rest = jnp.zeros((ROWS - REAL - 1, 128), jnp.bfloat16)
    packed = jnp.concatenate([head_rows, gain_row, rest], axis=0)
    packed = jnp.concatenate([packed[:16], packed[16:]], axis=1)
    mine = jnp.concatenate([columns, packed], axis=0)
    two = jnp.stack([mine, ring(mine, ("zh", "zl"), 16, -1)])
    return two, ring(two, ("zh", "zl"), 16, -2)


def first_spread(*slots):
    slots = jnp.concatenate(slots + slots)
    along_z = lax.dynamic_slice_in_dim(slots, (4 - lax.axis_index("zl")) % 4, 4, axis=0)
    return spread(along_z, True)


def unpack_kernel(parts_ref, head_ref, gain_ref):
    for x in range(4):
        for core in range(2):
            rows = parts_ref[x * 2 + core].astype(jnp.float32)
            place = core * 4 + x
            head_ref[place * REAL : (place + 1) * REAL, :] = rows[:REAL]
            if place == 0:
                gain_ref[...] = rows[REAL]


def reduce_shares(share):
    both = total(exchange(share, "core")).astype(jnp.bfloat16)
    plane = total(exchange(both.reshape(16, 4, ROWS, 128), ("x", "y"))).astype(jnp.bfloat16)
    spread = jnp.broadcast_to(plane[None], (4, 4, ROWS, 128)).reshape(16, ROWS, 128)
    line = total(exchange(spread, ("zh", "zl"))).astype(jnp.bfloat16)
    parts = exchange(jnp.broadcast_to(line[None], (PARTS, ROWS, 128)), ("x", "core"))
    head, gain = pl.pallas_call(
        unpack_kernel,
        out_shape=[jax.ShapeDtypeStruct((QUANTILES, 128), jnp.float32), jax.ShapeDtypeStruct((128,), jnp.float32)],
    )(parts)
    return head.T, gain


def local(queries, keys, values, resid, out_weight, head_weight, gain, doc_ids, prompt_lengths, targets):
    rows = queries.shape[1]
    core = lax.axis_index("core")
    place = (lax.axis_index("x") * 4 + lax.axis_index("zh")) * 2 + core
    own = jnp.concatenate([keys[0], values[0]], axis=1)
    far = ring(own, ("x", "zh"), 16, 1)
    slots = gather_z(out_weight, head_weight, gain)
    lines = lax.cond(place >= 0, first_spread, lambda *s: jnp.zeros((4, 4, BLOCK, CHUNK), jnp.bfloat16), *slots)
    plane = spread(lines, False).reshape(16, 4, BLOCK, CHUNK)
    near = ring(jnp.where(core == 0, own, far), "core", 2, 1)

    ids = doc_ids[0]
    first = place * rows
    query_ids = lax.dynamic_slice_in_dim(ids, first, rows)
    docs = jnp.arange(prompt_lengths.shape[1], dtype=jnp.int32)
    starts = jnp.sum((ids[None, :] < docs[:, None]).astype(jnp.int32), axis=1)
    onehot = (query_ids[:, None] == docs[None, :]).astype(jnp.int32)
    own_start = jnp.sum(onehot * starts[None, :], axis=1)
    own_prompt = jnp.sum(onehot * prompt_lengths[0][None, :], axis=1)
    query_pos = first + jnp.arange(rows, dtype=jnp.int32)
    live = (query_pos - own_start >= own_prompt).astype(jnp.float32)
    key_pos = first - SPAN * rows + jnp.arange((SPAN + 1) * rows, dtype=jnp.int32)
    allowed = (key_pos[None, :] >= own_start[:, None]) & (key_pos[None, :] <= query_pos[:, None])
    bias = jnp.where(allowed, 0.0, NEGATIVE).astype(jnp.float32)

    attended = attend(queries[0], 0, own, near, far, bias)
    kept, sent = project(core, attended, ring(attended, "core", 2, 1), plane)
    theta, token_grad, share = head_pass(core, kept, sent, ring(sent, "core", 2, 1), resid[0], targets, live[None, :])
    grad_head, grad_gain = reduce_shares(share)
    return theta.T[None], token_grad[None], grad_head, grad_gain


def solution(mesh):
    fine = Mesh(mesh.devices.reshape(EXTENT), AXES)
    ctx, dp = ("x", "zh", "core"), ("zl", "y")
    in_specs = (
        P(dp, ctx, None),
        P(dp, ctx, None),
        P(dp, ctx, None),
        P(dp, ctx, None),
        P(dp, None),
        P(dp, None),
        P(dp),
        P(dp, None),
        P(dp, None),
        P(dp, ctx),
    )
    out_specs = (P(dp, ctx, None), P(dp, ctx, None), P(dp, None), P(dp))
    return jax.shard_map(local, mesh=fine, in_specs=in_specs, out_specs=out_specs, check_vma=False)
```
